32 devices in a mesh: groups: 2 (over y), expert: 8 (over z, core), split: 2 (over x).
Axes of the slice: x: 2, y: 2, z: 4, core: 2. Of those that a mesh axis runs over, the one named last changes fastest.
Arguments:
- tokens: bfloat16 [512, 3584], P(('groups', 'expert', 'split')), parts along dimension 0, may hold values from -6 to 6
- expert_ids: int32 [512, 8], P(('groups', 'expert', 'split')), parts along dimension 0, may hold values from 0 to 15, all different within a row; in each aligned block of 16 rows (0 to 15, 16 to 31, ...) at most 8 rows name the same one
- gate_weights: float32 [512, 8], P(('groups', 'expert', 'split')), parts along dimension 0, may hold values from 0.1 to 0.5
- w_gate: bfloat16 [16, 3584, 1024], P('expert', None, 'split'), may hold values from -0.09375 to 0.09375
- w_up: bfloat16 [16, 3584, 1024], P('expert', None, 'split'), may hold values from -0.09375 to 0.09375
- w_down: bfloat16 [16, 1024, 3584], P('expert', 'split'), may hold values from -0.1875 to 0.1875
Outputs:
- mixed: bfloat16 [512, 3584], P(('groups', 'expert', 'split')), parts along dimension 0
The draws below stay inside these ranges and needn't reach their ends.
There are 2 independent parts, one for each index of `groups`. The reference program is written for one: setup_inputs(seed, part) draws one part's arguments, and reference() takes and returns one part's arrays. A program takes and returns all parts, laid end to end along the dimension named above; an argument that names none is the same for every part. Nothing has to cross between parts.
Inputs may be any that keep to these rules, and one draw needn't show every extreme that they name: `expert_ids`: each token names 8 different experts. Within the rows of one device no expert is named by more than 8 tokens, and in every draw some device has an expert named by exactly 8 of its tokens.
All inputs are finite; a program needn't handle non-finite values.
Results may differ from the reference program's by a relative error of at most 0.0065.
Values may be sent and summed in bfloat16 or wider, within the bound.
A program may use at most 64 MiB of HBM per device.

```python
import math
import jax
import jax.numpy as jnp
import numpy as np
from jax import lax

D = 3584
FF = 1024
TOPK = 8
TOK_DEV = 16
EXPERTS = 16
CAP = 8
TOKENS = 256
N_EXPERT = 8
N_SPLIT = 2


def level_of(rng, dims, cuts, smallest, high):
    def one(dim, parts):
        heights = jax.random.uniform(jax.random.fold_in(jax.random.fold_in(rng, 6), dim), (parts,), jnp.float32, smallest / len(cuts), high / len(cuts))
        return jnp.repeat(jnp.exp(heights), dims[dim] // parts).reshape((-1,) + (1,) * (len(dims) - dim - 1))

    level = one(*cuts[0])
    for cut in cuts[1:]:
        level = level * one(*cut)
    return level


def assign_block(own_key, own, number, rows, number_of, top, bound, slope):
    sequence = jax.random.permutation(own_key, number_of)
    crowded, ordinary = shares(number_of, rows * top, bound, slope, True), shares(number_of, rows * top, bound, slope, False)
    places = jnp.arange(number_of)

    def named(tallies, offset_by):
        used = int((tallies > 0).sum())
        fixed = max(1, used // 4)
        passed = fixed + (places - fixed + offset_by * (used - fixed)) % max(1, number_of - fixed)
        return jnp.zeros((number_of,), jnp.int32).at[sequence[jnp.where(places < fixed, places, passed)]].set(jnp.asarray(tallies, jnp.int32))

    tallies = jnp.where(number % 4 == 0, named(crowded, number // 4), named(ordinary, number - number // 4 - 1))
    mixed = jax.random.permutation(jax.random.fold_in(own, 3), number_of)
    source_of, taker = mixed[0:number_of // 2 * 2:2], mixed[1:number_of // 2 * 2:2]
    room = jnp.minimum(tallies[source_of] - 1, bound - tallies[taker]) // 2
    room = jnp.where((source_of == sequence[0]) | (taker == sequence[0]) | (tallies[taker] == 0), 0, jnp.maximum(room, 0))
    passed = jax.random.randint(jax.random.fold_in(own, 4), (number_of // 2,), 0, 1 << 20) % (room + 1)
    tallies = tallies.at[source_of].add(-passed).at[taker].add(passed)
    members = jnp.searchsorted(jnp.cumsum(tallies), jnp.arange(rows * top), side="right").astype(jnp.int32)
    table = members.reshape(top, rows).T
    table = table[jax.random.permutation(jax.random.fold_in(own, 1), rows)]
    offset_by = jax.random.randint(jax.random.fold_in(own, 2), (rows, 1), 0, top)
    return jnp.take_along_axis(table, (jnp.arange(top)[None, :] + offset_by) % top, axis=1)


def shares(amount, total, reach, skew, full):
    loads = [(1 << 20) // math.isqrt(rank ** skew) + 1 for rank in range(1, amount + 1)]
    largest = reach if full else min(reach, max(-(-total // amount), total * loads[0] // sum(loads)))
    least = 1 if total - largest >= amount - 1 else 0
    given, rest = [largest] + [least] * (amount - 1), total - largest - least * (amount - 1)
    while rest > 0:
        free = [i for i in range(1, amount) if given[i] < largest] or [i for i in range(1, amount) if given[i] < reach]
        pool, remaining = sum([loads[i] for i in free]), rest
        for i in free:
            extra = min(reach - given[i], max(1, remaining * loads[i] // pool), rest)
            given[i] = given[i] + extra
            rest = rest - extra
    return np.array(given)


def gaussian(stream_key, dims, scale, bound, split=(), kind=jnp.bfloat16):
    factor_of = level_of(stream_key, dims, split, -0.22, 0.18) if split else 1.0
    values = jax.random.normal(stream_key, dims, jnp.float32) * scale * factor_of
    return jnp.minimum(jnp.maximum(values, -bound), bound).astype(kind)


def setup_inputs(seed: int = 0, part: int = 0) -> dict:
    splits = jax.random.split(jax.random.key(seed), 7)
    part_splits = jax.random.split(jax.random.fold_in(splits[6], part), 7)
    tokens = gaussian(part_splits[0], (TOKENS, D), 1.0, 6.0, ((0, 16),))
    expert_ids_keys = jax.random.split(jax.random.fold_in(part_splits[1], 1), TOKENS // TOK_DEV)
    expert_ids_turns = jax.random.permutation(jax.random.fold_in(part_splits[1], 3), TOKENS // TOK_DEV)
    expert_ids = jax.vmap(lambda own, number: assign_block(jax.random.fold_in(part_splits[1], 2), own, number, TOK_DEV, EXPERTS, TOPK, CAP, 2))(expert_ids_keys, expert_ids_turns).reshape((TOKENS, TOPK))
    gate_weights = jnp.clip(0.1 + 0.4 * jax.random.uniform(part_splits[2], (TOKENS, TOPK), jnp.float32) ** level_of(part_splits[2], (TOKENS, TOPK), ((0, 16),), -0.2, 0.2), 0.1, 0.5)
    w_gate = gaussian(splits[3], (EXPERTS, D, FF), D ** -0.5, 0.09375, ((0, 8), (2, 2)))
    w_up = gaussian(splits[4], (EXPERTS, D, FF), D ** -0.5, 0.09375, ((0, 8), (2, 2)))
    w_down = gaussian(splits[5], (EXPERTS, FF, D), FF ** -0.5, 0.1875, ((0, 8), (1, 2)))
    return dict(tokens=tokens, expert_ids=expert_ids, gate_weights=gate_weights, w_gate=w_gate, w_up=w_up, w_down=w_down)


def slot_targets(chosen_ids, capacity, expert_total):
    flat_ids = chosen_ids.reshape(-1)
    chosen = (flat_ids[:, None] == jnp.arange(expert_total, dtype=jnp.int32)[None, :]).astype(jnp.int32)
    earlier = jnp.cumsum(chosen, axis=0) - chosen
    slot_index = jnp.sum(earlier * chosen, axis=1).astype(jnp.int32)
    return (flat_ids * capacity + slot_index).reshape(chosen_ids.shape).astype(jnp.int32)


def reference(tokens, expert_ids, gate_weights, w_gate, w_up, w_down):
    device_count = N_EXPERT * N_SPLIT
    token_rows = tokens.reshape(device_count, TOK_DEV, D)
    chosen_ids = expert_ids.reshape(device_count, TOK_DEV, TOPK)
    destination = jax.vmap(lambda ids_block: slot_targets(ids_block, CAP, EXPERTS))(chosen_ids)

    def fill_slots(pair):
        block_rows, block_dest = pair
        selector = jnp.any(jnp.arange(EXPERTS * CAP, dtype=jnp.int32)[:, None, None] == block_dest[None, :, :], axis=-1)
        filled = jnp.dot(selector.astype(jnp.bfloat16), block_rows, preferred_element_type=jnp.float32)
        return filled.astype(jnp.bfloat16).reshape(EXPERTS, CAP, D)

    buffers = lax.map(fill_slots, (token_rows, destination))
    quarter = FF // N_SPLIT

    def run_expert(pack):
        index, gate_mat, up_mat, down_mat = pack
        row_block = lax.dynamic_index_in_dim(buffers, index, 1, keepdims=False).reshape(device_count * CAP, D)
        gate_act = jnp.dot(row_block, gate_mat, preferred_element_type=jnp.float32)
        up_act = jnp.dot(row_block, up_mat, preferred_element_type=jnp.float32)
        hidden = (jax.nn.silu(gate_act) * up_act).astype(jnp.bfloat16)
        hidden_q = hidden.reshape(device_count * CAP, N_SPLIT, quarter).astype(jnp.float32)
        down_q = down_mat.reshape(N_SPLIT, quarter, D).astype(jnp.float32)
        partial_value = jnp.einsum('nqf,qfd->qnd', hidden_q, down_q)
        partial_value = lax.optimization_barrier(partial_value.astype(jnp.bfloat16)).astype(jnp.float32)
        return jnp.sum(partial_value, axis=0).astype(jnp.bfloat16).reshape(device_count, CAP, D)

    outputs = lax.map(run_expert, (jnp.arange(EXPERTS, dtype=jnp.int32), w_gate, w_up, w_down))
    slot_index = (destination - chosen_ids * CAP).astype(jnp.int32)
    device_index = jnp.arange(device_count, dtype=jnp.int32)[:, None, None]
    picked = outputs[chosen_ids, device_index, slot_index].astype(jnp.float32)
    weights = gate_weights.reshape(device_count, TOK_DEV, TOPK)
    mixed = jnp.sum(weights[..., None] * picked, axis=2)
    return mixed.astype(jnp.bfloat16).reshape(TOKENS, D)
```

```python
import jax
import jax.numpy as jnp
from jax import lax
from jax.experimental import pallas as pl
from jax.experimental.pallas import tpu as pltpu
from jax.sharding import PartitionSpec as P


def slot_targets(chosen_ids, capacity, expert_total):
    flat_ids = chosen_ids.reshape(-1)
    chosen = (flat_ids[:, None] == jnp.arange(expert_total, dtype=jnp.int32)[None, :]).astype(
        jnp.int32
    )
    earlier = jnp.cumsum(chosen, axis=0) - chosen
    slot_index = jnp.sum(earlier * chosen, axis=1)
    return (flat_ids * capacity + slot_index).reshape(chosen_ids.shape)


def shards(tokens, expert_ids, gate_weights, w_gate, w_up, w_down):
    expert_count = lax.axis_size("expert")
    local_count = w_gate.shape[0]
    expert_total = local_count * expert_count
    width = tokens.shape[1]
    capacity = max(3, tokens.shape[0] * expert_ids.shape[1] // expert_total)
    destination = slot_targets(expert_ids, capacity, expert_total)
    slot_range = jnp.arange(expert_total * capacity, dtype=jnp.int32)
    matches = slot_range[:, None, None] == destination[None, :, :]
    selector = jnp.any(matches, axis=-1).astype(jnp.bfloat16)
    send_buffer = jnp.dot(selector, tokens, preferred_element_type=jnp.float32).astype(jnp.bfloat16)
    send_buffer = send_buffer.reshape(expert_total, capacity, width)

    def run_experts(piece, start=0):
        block_shape = piece.shape
        row_block = piece.reshape(-1, local_count, capacity, width)
        gate_act = jnp.einsum(
            "mjcd,jdf->mjcf", row_block, w_gate, preferred_element_type=jnp.float32
        )
        up_act = jnp.einsum("mjcd,jdf->mjcf", row_block, w_up, preferred_element_type=jnp.float32)
        hidden = (jax.nn.silu(gate_act) * up_act).astype(jnp.bfloat16)
        partial_value = jnp.einsum(
            "mjcf,jfd->mjcd", hidden, w_down, preferred_element_type=jnp.float32
        )
        return partial_value.astype(jnp.bfloat16).reshape(block_shape)

    arrived = lax.all_to_all(send_buffer, "expert", split_axis=0, concat_axis=0, tiled=True)
    arrived = arrived.reshape(expert_count, 1, local_count, capacity, width)
    partial_value = run_experts(lax.all_gather(arrived, "split", axis=1, tiled=True), jnp.int32(0))
    summed = lax.psum_scatter(
        partial_value.astype(jnp.float32).astype(jnp.bfloat16),
        "split",
        scatter_dimension=1,
        tiled=True,
    )
    expert_out = summed.reshape(expert_total, capacity, width)
    returned = lax.all_to_all(expert_out, "expert", split_axis=0, concat_axis=0, tiled=True)
    combiner = jnp.sum(jnp.where(matches, gate_weights[None, :, :], 0.0), axis=-1).T
    mixed = jnp.dot(
        combiner,
        returned.reshape(expert_total * capacity, width).astype(jnp.float32),
        precision=lax.Precision.HIGHEST,
        preferred_element_type=jnp.float32,
    )
    return mixed.astype(jnp.bfloat16)


CHUNK = 512
LANES = 128


def fused_kernel(
    tok_ref, ids_ref, gw_ref, wg_hbm, wu_hbm, wd_hbm, out_ref,
    xg, ext, wg, wu, wd, acc_g, acc_u, hid, cw, y, s1, r1, s2, r2, s3, r3,
    wg_sem, wu_sem, wd_sem,
    ezs, ezr, exs, exr, ecs, ecr,
    zs, zr, xs, xr, cs, cr,
    s1s, s1r, s2s, s2r, s3s, s3r,
):
    T, width = tok_ref.shape
    local_count, _, part = wg.shape
    nz = lax.axis_size("expert") // 2
    steps = width // CHUNK
    line = nz * T
    half = 2 * line
    e_idx = lax.axis_index("expert")
    x_idx = lax.axis_index("split")
    z, core = e_idx // 2, lax.rem(e_idx, 2)
    core_peer = {"expert": z * 2 + (1 - core), "split": x_idx}
    x_peer = {"expert": e_idx, "split": 1 - x_idx}

    def z_at(offset):
        return lax.rem(z + (offset % nz), nz)

    def z_peer(offset):
        return {"expert": z_at(offset) * 2 + core, "split": x_idx}

    def cols(c):
        return pl.ds(pl.multiple_of(c * CHUNK, CHUNK), CHUNK)

    def rows(index, base=0):
        return pl.ds(pl.multiple_of(base + index * T, T), T)

    def remote(src, dst, send, recv, peer):
        return pltpu.make_async_remote_copy(
            src_ref=src, dst_ref=dst, send_sem=send, recv_sem=recv,
            device_id=peer, device_id_type=pl.DeviceIdType.MESH,
        )

    def w_copy(c):
        return (
            pltpu.make_async_copy(wg_hbm.at[:, cols(c), :], wg.at[:, cols(c), :], wg_sem.at[c]),
            pltpu.make_async_copy(wu_hbm.at[:, cols(c), :], wu.at[:, cols(c), :], wu_sem.at[c]),
        )

    wd_copy = pltpu.make_async_copy(wd_hbm, wd, wd_sem)

    barrier = pltpu.get_barrier_semaphore()
    peers = [core_peer, x_peer] + [z_peer(d) for d in range(1, nz)]
    for peer in peers:
        pl.semaphore_signal(barrier, inc=1, device_id=peer, device_id_type=pl.DeviceIdType.MESH)

    @pl.loop(0, steps)
    def _(c):
        for copy in w_copy(c):
            copy.start()

    wd_copy.start()

    own = rows(z)
    xg[own, :] = tok_ref[...]
    lane = lax.broadcasted_iota(jnp.int32, (T, LANES), 1)
    table = jnp.zeros((T, LANES), jnp.float32)
    for k in range(ids_ref.shape[1]):
        table = table + jnp.where(ids_ref[:, k : k + 1] == lane, gw_ref[:, k : k + 1], 0.0)
    ext[own, :] = table
    acc_g[...] = jnp.zeros_like(acc_g)
    acc_u[...] = jnp.zeros_like(acc_u)
    pl.semaphore_wait(barrier, len(peers))

    def gz(buf, where, send, recv, d, arriving):
        block = buf.at[(rows(z_at(-d)) if arriving else own,) + where]
        return remote(block, block, send.at[d], recv.at[d], z_peer(d))

    def gx(buf, where, send, recv, d, arriving):
        index = z_at(-d)
        src = buf.at[(rows(index),) + where]
        dst = buf.at[(rows(index, line),) + where]
        if arriving:
            src = dst
        return remote(src, dst, send.at[d], recv.at[d], x_peer)

    def gc(buf, where, send, recv, side, arriving):
        src = buf.at[(pl.ds(side * line, line),) + where]
        dst = buf.at[(pl.ds(half + side * line, line),) + where]
        if arriving:
            src = dst
        return remote(src, dst, send.at[side], recv.at[side], core_peer)

    e_where = (slice(None),)

    def e_args(send, recv):
        return ext, e_where, send, recv

    def c_args(c, send, recv):
        return xg, (cols(c),), send.at[c], recv.at[c]

    def first_sends(za, xa):
        for d in range(1, nz):
            gz(*za, d, False).start()
        gx(*xa, 0, False).start()

    def forward_line(za, xa, ca):
        for d in range(1, nz):
            gz(*za, d, True).wait_recv()
            gx(*xa, d, False).start()
        gc(*ca, 0, False).start()

    def forward_other(xa, ca):
        for d in range(nz):
            gx(*xa, d, True).wait_recv()
        gc(*ca, 1, False).start()

    def from_core(ca):
        for side in range(2):
            gc(*ca, side, True).wait_recv()

    def gather_sent(za, xa, ca):
        for d in range(1, nz):
            gz(*za, d, False).wait_send()
        for d in range(nz):
            gx(*xa, d, False).wait_send()
        for side in range(2):
            gc(*ca, side, False).wait_send()

    ez, ex, ec = e_args(ezs, ezr), e_args(exs, exr), e_args(ecs, ecr)
    first_sends(ez, ex)

    @pl.loop(0, steps)
    def _(c):
        first_sends(c_args(c, zs, zr), c_args(c, xs, xr))

    forward_line(ez, ex, ec)

    @pl.loop(0, steps + 2)
    def _(i):
        @pl.when(i < steps)
        def _():
            forward_line(c_args(i, zs, zr), c_args(i, xs, xr), c_args(i, cs, cr))

        @pl.when((i >= 1) & (i < steps + 1))
        def _():
            forward_other(c_args(i - 1, xs, xr), c_args(i - 1, cs, cr))

        @pl.when(i >= 2)
        def _():
            c = i - 2
            from_core(c_args(c, cs, cr))
            for copy in w_copy(c):
                copy.wait()
            value = xg[:, cols(c)]
            for j in range(local_count):
                acc_g[j] += jnp.dot(value, wg[j, cols(c), :], preferred_element_type=jnp.float32)
                acc_u[j] += jnp.dot(value, wu[j, cols(c), :], preferred_element_type=jnp.float32)

    forward_other(ex, ec)
    for j in range(local_count):
        gate = acc_g[j]
        hid[j] = (gate / (1.0 + jnp.exp(-gate)) * acc_u[j]).astype(jnp.bfloat16)
    from_core(ec)
    lanes = lax.broadcasted_iota(jnp.int32, (2 * half, LANES), 1)
    for j in range(local_count):
        chosen = jnp.where(lanes == e_idx * local_count + j, ext[...], 0.0)
        cw[j] = jnp.broadcast_to(jnp.sum(chosen, axis=1, keepdims=True), (2 * half, LANES))
    wd_copy.wait()

    def rc(c):
        return remote(s1.at[:, cols(c)], r1.at[:, cols(c)], s1s.at[c], s1r.at[c], core_peer)

    def rx(c):
        return remote(s2.at[:, cols(c)], r2.at[:, cols(c)], s2s.at[c], s2r.at[c], x_peer)

    def rz(c, d):
        return remote(
            s3.at[rows(z_at(d)), cols(c)], r3.at[d, :, cols(c)],
            s3s.at[c, d], s3r.at[c, d], z_peer(d),
        )

    lag_x, lag_z, lag_out = 1, 3, 5

    @pl.loop(0, steps + lag_out)
    def _(i):
        @pl.when(i < steps)
        def _():
            total = None
            for j in range(local_count):
                value = jnp.dot(hid[j], wd[j, :, cols(i)], preferred_element_type=jnp.float32)
                value = value * jnp.concatenate([cw[j]] * (CHUNK // LANES), axis=1)
                total = value if total is None else total + value
            s1[:, cols(i)] = total[half:].astype(jnp.bfloat16)
            y[:, cols(i)] = total[:half]
            rc(i).start()

        @pl.when((i >= lag_x) & (i < steps + lag_x))
        def _():
            c = i - lag_x
            rc(c).wait_recv()
            total = y[:, cols(c)] + r1[:, cols(c)].astype(jnp.float32)
            s2[:, cols(c)] = total[line:].astype(jnp.bfloat16)
            y[:line, cols(c)] = total[:line]
            rx(c).start()

        @pl.when((i >= lag_z) & (i < steps + lag_z))
        def _():
            c = i - lag_z
            rx(c).wait_recv()
            total = y[:line, cols(c)] + r2[:, cols(c)].astype(jnp.float32)
            s3[:, cols(c)] = total.astype(jnp.bfloat16)
            y[:line, cols(c)] = total
            for d in range(1, nz):
                rz(c, d).start()

        @pl.when(i >= lag_out)
        def _():
            c = i - lag_out
            total = y[own, cols(c)]
            for d in range(1, nz):
                rz(c, d).wait_recv()
                total = total + r3[d, :, cols(c)].astype(jnp.float32)
            out_ref[:, cols(c)] = total.astype(out_ref.dtype)

    gather_sent(ez, ex, ec)

    @pl.loop(0, steps)
    def _(c):
        gather_sent(c_args(c, zs, zr), c_args(c, xs, xr), c_args(c, cs, cr))
        rc(c).wait_send()
        rx(c).wait_send()
        for d in range(1, nz):
            rz(c, d).wait_send()


def fused_shards(tokens, expert_ids, gate_weights, w_gate, w_up, w_down):
    T, width = tokens.shape
    local_count, _, part = w_gate.shape
    nz = lax.axis_size("expert") // 2
    steps = width // CHUNK
    line = nz * T
    half, total = 2 * line, 4 * line
    bf16, f32 = jnp.bfloat16, jnp.float32
    dma = pltpu.SemaphoreType.DMA
    vmem = pl.BlockSpec(memory_space=pltpu.VMEM)
    hbm = pl.BlockSpec(memory_space=pl.ANY)
    flops = 2 * total * width * part * local_count * 3
    return pl.pallas_call(
        fused_kernel,
        out_shape=jax.ShapeDtypeStruct((T, width), bf16),
        in_specs=[vmem] * 3 + [hbm] * 3,
        out_specs=vmem,
        scratch_shapes=[
            pltpu.VMEM((total, width), bf16),
            pltpu.VMEM((total, LANES), f32),
            pltpu.VMEM(w_gate.shape, bf16),
            pltpu.VMEM(w_up.shape, bf16),
            pltpu.VMEM(w_down.shape, bf16),
            pltpu.VMEM((local_count, total, part), f32),
            pltpu.VMEM((local_count, total, part), f32),
            pltpu.VMEM((local_count, total, part), bf16),
            pltpu.VMEM((local_count, total, LANES), f32),
            pltpu.VMEM((half, width), f32),
            pltpu.VMEM((half, width), bf16),
            pltpu.VMEM((half, width), bf16),
            pltpu.VMEM((line, width), bf16),
            pltpu.VMEM((line, width), bf16),
            pltpu.VMEM((line, width), bf16),
            pltpu.VMEM((nz, T, width), bf16),
            dma((steps,)),
            dma((steps,)),
            dma,
            *[dma((nz,)), dma((nz,)), dma((nz,)), dma((nz,)), dma((2,)), dma((2,))],
            *[dma((steps, nz))] * 4,
            *[dma((steps, 2))] * 2,
            *[dma((steps,))] * 4,
            *[dma((steps, nz))] * 2,
        ],
        compiler_params=pltpu.CompilerParams(
            collective_id=0, has_side_effects=True, vmem_limit_bytes=50 * 1024 * 1024
        ),
        cost_estimate=pl.CostEstimate(
            flops=flops,
            bytes_accessed=2 * (w_gate.size + w_up.size + w_down.size),
            transcendentals=total * part * local_count,
        ),
    )(tokens, expert_ids, gate_weights, w_gate, w_up, w_down)


def pick(mesh):
    def body(tokens, expert_ids, gate_weights, w_gate, w_up, w_down):
        expert_count = mesh.shape["expert"]
        rows = tokens.shape[0] * expert_count * mesh.shape["split"]
        fits = (
            mesh.shape["split"] == 2
            and expert_count % 2 == 0
            and rows <= 256
            and tokens.shape[0] % 16 == 0
            and tokens.shape[1] % CHUNK == 0
            and w_gate.shape[0] * expert_count <= LANES
        )
        run = fused_shards if fits else shards
        return run(tokens, expert_ids, gate_weights, w_gate, w_up, w_down)

    return body


def solution(mesh):
    in_specs = (
        P(("groups", "expert", "split"), None),
        P(("groups", "expert", "split"), None),
        P(("groups", "expert", "split"), None),
        P("expert", None, "split"),
        P("expert", None, "split"),
        P("expert", "split", None),
    )
    out_specs = P(("groups", "expert", "split"), None)
    return jax.shard_map(pick(mesh), mesh=mesh, in_specs=in_specs, out_specs=out_specs, check_vma=False)
```

```python
import jax
import jax.numpy as jnp
from jax import lax
from jax.experimental import pallas as pl
from jax.experimental.pallas import tpu as pltpu
from jax.sharding import PartitionSpec as P


def slot_targets(chosen_ids, capacity, expert_total):
    flat_ids = chosen_ids.reshape(-1)
    chosen = (flat_ids[:, None] == jnp.arange(expert_total, dtype=jnp.int32)[None, :]).astype(
        jnp.int32
    )
    earlier = jnp.cumsum(chosen, axis=0) - chosen
    slot_index = jnp.sum(earlier * chosen, axis=1)
    return (flat_ids * capacity + slot_index).reshape(chosen_ids.shape)


def shards(tokens, expert_ids, gate_weights, w_gate, w_up, w_down):
    expert_count = lax.axis_size("expert")
    local_count = w_gate.shape[0]
    expert_total = local_count * expert_count
    width = tokens.shape[1]
    capacity = max(3, tokens.shape[0] * expert_ids.shape[1] // expert_total)
    destination = slot_targets(expert_ids, capacity, expert_total)
    slot_range = jnp.arange(expert_total * capacity, dtype=jnp.int32)
    matches = slot_range[:, None, None] == destination[None, :, :]
    selector = jnp.any(matches, axis=-1).astype(jnp.bfloat16)
    send_buffer = jnp.dot(selector, tokens, preferred_element_type=jnp.float32).astype(jnp.bfloat16)
    send_buffer = send_buffer.reshape(expert_total, capacity, width)

    def run_experts(piece, start=0):
        block_shape = piece.shape
        row_block = piece.reshape(-1, local_count, capacity, width)
        gate_act = jnp.einsum(
            "mjcd,jdf->mjcf", row_block, w_gate, preferred_element_type=jnp.float32
        )
        up_act = jnp.einsum("mjcd,jdf->mjcf", row_block, w_up, preferred_element_type=jnp.float32)
        hidden = (jax.nn.silu(gate_act) * up_act).astype(jnp.bfloat16)
        partial_value = jnp.einsum(
            "mjcf,jfd->mjcd", hidden, w_down, preferred_element_type=jnp.float32
        )
        return partial_value.astype(jnp.bfloat16).reshape(block_shape)

    arrived = lax.all_to_all(send_buffer, "expert", split_axis=0, concat_axis=0, tiled=True)
    arrived = arrived.reshape(expert_count, 1, local_count, capacity, width)
    partial_value = run_experts(lax.all_gather(arrived, "split", axis=1, tiled=True), jnp.int32(0))
    summed = lax.psum_scatter(
        partial_value.astype(jnp.float32).astype(jnp.bfloat16),
        "split",
        scatter_dimension=1,
        tiled=True,
    )
    expert_out = summed.reshape(expert_total, capacity, width)
    returned = lax.all_to_all(expert_out, "expert", split_axis=0, concat_axis=0, tiled=True)
    combiner = jnp.sum(jnp.where(matches, gate_weights[None, :, :], 0.0), axis=-1).T
    mixed = jnp.dot(
        combiner,
        returned.reshape(expert_total * capacity, width).astype(jnp.float32),
        precision=lax.Precision.HIGHEST,
        preferred_element_type=jnp.float32,
    )
    return mixed.astype(jnp.bfloat16)


GATHER = 896
REDUCE = 896
AHEAD = 1
LAGS = (1, 3, 5)
LANES = 128


def fused_kernel(
    tok_hbm, ids_hbm, gw_hbm, wg_hbm, wu_hbm, wd_hbm, out_ref,
    xg, ext, ids_ref, gw_ref, wg, wu, wd, acc_g, acc_u, hid, cw, y, s1, r1, s2, r2, s3, r3,
    tok_sem, ids_sem, gw_sem, wg_sem, wu_sem, wd_sem,
    ezs, ezr, exs, exr, ecs, ecr,
    zs, zr, xs, xr, cs, cr,
    s1s, s1r, s2s, s2r, s3s, s3r,
):
    T, width = tok_hbm.shape
    local_count, _, part = wg.shape
    nz = lax.axis_size("expert") // 2
    steps, reduce_steps = width // GATHER, width // REDUCE
    line = nz * T
    half = 2 * line
    e_idx = lax.axis_index("expert")
    x_idx = lax.axis_index("split")
    z, core = e_idx // 2, lax.rem(e_idx, 2)
    core_peer = {"expert": z * 2 + (1 - core), "split": x_idx}
    x_peer = {"expert": e_idx, "split": 1 - x_idx}

    def z_at(offset):
        return lax.rem(z + (offset % nz), nz)

    def z_peer(offset):
        return {"expert": z_at(offset) * 2 + core, "split": x_idx}

    def cols(c, size=GATHER):
        return pl.ds(pl.multiple_of(c * size, size), size)

    def rows(index, base=0):
        return pl.ds(pl.multiple_of(base + index * T, T), T)

    def remote(src, dst, send, recv, peer):
        return pltpu.make_async_remote_copy(
            src_ref=src, dst_ref=dst, send_sem=send, recv_sem=recv,
            device_id=peer, device_id_type=pl.DeviceIdType.MESH,
        )

    own = rows(z)
    tok_copy = pltpu.make_async_copy(tok_hbm, xg.at[own, :], tok_sem)
    ids_copy = pltpu.make_async_copy(ids_hbm, ids_ref, ids_sem)
    gw_copy = pltpu.make_async_copy(gw_hbm, gw_ref, gw_sem)
    for copy in (ids_copy, gw_copy, tok_copy):
        copy.start()

    def w_copy(c):
        return (
            pltpu.make_async_copy(wg_hbm.at[:, cols(c), :], wg.at[:, cols(c), :], wg_sem.at[c]),
            pltpu.make_async_copy(wu_hbm.at[:, cols(c), :], wu.at[:, cols(c), :], wu_sem.at[c]),
        )

    wd_copy = pltpu.make_async_copy(wd_hbm, wd, wd_sem)

    barrier = pltpu.get_barrier_semaphore()
    peers = [core_peer, x_peer] + [z_peer(d) for d in range(1, nz)]
    for peer in peers:
        pl.semaphore_signal(barrier, inc=1, device_id=peer, device_id_type=pl.DeviceIdType.MESH)

    @pl.loop(0, steps)
    def _(c):
        for copy in w_copy(c):
            copy.start()

    wd_copy.start()

    acc_g[...] = jnp.zeros_like(acc_g)
    acc_u[...] = jnp.zeros_like(acc_u)
    ids_copy.wait()
    gw_copy.wait()
    ids, weights = jnp.transpose(ids_ref[...]), jnp.transpose(gw_ref[...])
    lane = lax.broadcasted_iota(jnp.int32, (T, LANES), 1)
    table = jnp.zeros((T, LANES), jnp.float32)
    for k in range(ids.shape[1]):
        table = table + jnp.where(ids[:, k : k + 1] == lane, weights[:, k : k + 1], 0.0)
    ext[own, :] = table
    tok_copy.wait()
    pl.semaphore_wait(barrier, len(peers))

    def gz(buf, where, send, recv, d, arriving):
        block = buf.at[(rows(z_at(-d)) if arriving else own,) + where]
        return remote(block, block, send.at[d], recv.at[d], z_peer(d))

    def gx(buf, where, send, recv, d, arriving):
        index = z_at(-d)
        src = buf.at[(rows(index),) + where]
        dst = buf.at[(rows(index, line),) + where]
        if arriving:
            src = dst
        return remote(src, dst, send.at[d], recv.at[d], x_peer)

    def gc(buf, where, send, recv, side, arriving):
        src = buf.at[(pl.ds(side * line, line),) + where]
        dst = buf.at[(pl.ds(half + side * line, line),) + where]
        if arriving:
            src = dst
        return remote(src, dst, send.at[side], recv.at[side], core_peer)

    e_where = (slice(None),)

    def e_args(send, recv):
        return ext, e_where, send, recv

    def c_args(c, send, recv):
        return xg, (cols(c),), send.at[c], recv.at[c]

    def first_sends(za, xa):
        for d in range(1, nz):
            gz(*za, d, False).start()
        gx(*xa, 0, False).start()

    def forward_line(za, xa, ca):
        for d in range(1, nz):
            gz(*za, d, True).wait_recv()
            gx(*xa, d, False).start()
        gc(*ca, 0, False).start()

    def forward_other(xa, ca):
        for d in range(nz):
            gx(*xa, d, True).wait_recv()
        gc(*ca, 1, False).start()

    def from_core(ca):
        for side in range(2):
            gc(*ca, side, True).wait_recv()

    def gather_sent(za, xa, ca):
        for d in range(1, nz):
            gz(*za, d, False).wait_send()
        for d in range(nz):
            gx(*xa, d, False).wait_send()
        for side in range(2):
            gc(*ca, side, False).wait_send()

    ez, ex, ec = e_args(ezs, ezr), e_args(exs, exr), e_args(ecs, ecr)
    first_sends(ez, ex)

    for c in range(AHEAD):
        first_sends(c_args(c, zs, zr), c_args(c, xs, xr))
    forward_line(ez, ex, ec)

    @pl.loop(0, steps + 2)
    def _(i):
        @pl.when(i + AHEAD < steps)
        def _():
            first_sends(c_args(i + AHEAD, zs, zr), c_args(i + AHEAD, xs, xr))

        @pl.when(i < steps)
        def _():
            forward_line(c_args(i, zs, zr), c_args(i, xs, xr), c_args(i, cs, cr))

        @pl.when((i >= 1) & (i < steps + 1))
        def _():
            forward_other(c_args(i - 1, xs, xr), c_args(i - 1, cs, cr))

        @pl.when(i == 1)
        def _():
            forward_other(ex, ec)

        @pl.when(i == 2)
        def _():
            from_core(ec)
            lanes = lax.broadcasted_iota(jnp.int32, (2 * half, LANES), 1)
            for j in range(local_count):
                chosen = jnp.where(lanes == e_idx * local_count + j, ext[...], 0.0)
                weight = jnp.sum(chosen, axis=1, keepdims=True)
                cw[j] = jnp.broadcast_to(weight, (2 * half, LANES))

        @pl.when(i >= 2)
        def _():
            c = i - 2
            from_core(c_args(c, cs, cr))
            for copy in w_copy(c):
                copy.wait()
            value = xg[:, cols(c)]
            for j in range(local_count):
                acc_g[j] += jnp.dot(value, wg[j, cols(c), :], preferred_element_type=jnp.float32)
                acc_u[j] += jnp.dot(value, wu[j, cols(c), :], preferred_element_type=jnp.float32)

    for j in range(local_count):
        gate = acc_g[j]
        hid[j] = (gate / (1.0 + jnp.exp(-gate)) * acc_u[j]).astype(jnp.bfloat16)
    wd_copy.wait()

    def rc(c):
        return remote(s1.at[:, cols(c, REDUCE)], r1.at[:, cols(c, REDUCE)], s1s.at[c], s1r.at[c], core_peer)

    def rx(c):
        return remote(s2.at[:, cols(c, REDUCE)], r2.at[:, cols(c, REDUCE)], s2s.at[c], s2r.at[c], x_peer)

    def rz(c, d):
        return remote(
            s3.at[rows(z_at(d)), cols(c, REDUCE)], r3.at[d, :, cols(c, REDUCE)],
            s3s.at[c, d], s3r.at[c, d], z_peer(d),
        )

    lag_x, lag_z, lag_out = LAGS

    @pl.loop(0, reduce_steps + lag_out)
    def _(i):
        @pl.when(i < reduce_steps)
        def _():
            total = None
            for j in range(local_count):
                value = jnp.dot(hid[j], wd[j, :, cols(i, REDUCE)], preferred_element_type=jnp.float32)
                value = value * jnp.concatenate([cw[j]] * (REDUCE // LANES), axis=1)
                total = value if total is None else total + value
            s1[:, cols(i, REDUCE)] = total[half:].astype(jnp.bfloat16)
            y[:, cols(i, REDUCE)] = total[:half]
            rc(i).start()

        @pl.when((i >= lag_x) & (i < reduce_steps + lag_x))
        def _():
            c = i - lag_x
            rc(c).wait_recv()
            total = y[:, cols(c, REDUCE)] + r1[:, cols(c, REDUCE)].astype(jnp.float32)
            s2[:, cols(c, REDUCE)] = total[line:].astype(jnp.bfloat16)
            y[:line, cols(c, REDUCE)] = total[:line]
            rx(c).start()

        @pl.when((i >= lag_z) & (i < reduce_steps + lag_z))
        def _():
            c = i - lag_z
            rx(c).wait_recv()
            total = y[:line, cols(c, REDUCE)] + r2[:, cols(c, REDUCE)].astype(jnp.float32)
            s3[:, cols(c, REDUCE)] = total.astype(jnp.bfloat16)
            y[:line, cols(c, REDUCE)] = total
            for d in range(1, nz):
                rz(c, d).start()

        @pl.when(i >= lag_out)
        def _():
            c = i - lag_out
            total = y[own, cols(c, REDUCE)]
            for d in range(1, nz):
                rz(c, d).wait_recv()
                total = total + r3[d, :, cols(c, REDUCE)].astype(jnp.float32)
            out_ref[:, cols(c, REDUCE)] = total.astype(out_ref.dtype)
            rc(c).wait_send()
            rx(c).wait_send()
            for d in range(1, nz):
                rz(c, d).wait_send()

        @pl.when(i < steps)
        def _():
            gather_sent(c_args(i, zs, zr), c_args(i, xs, xr), c_args(i, cs, cr))

    gather_sent(ez, ex, ec)


def fused_shards(tokens, expert_ids, gate_weights, w_gate, w_up, w_down):
    T, width = tokens.shape
    local_count, _, part = w_gate.shape
    nz = lax.axis_size("expert") // 2
    steps, reduce_steps = width // GATHER, width // REDUCE
    line = nz * T
    half, total = 2 * line, 4 * line
    bf16, f32 = jnp.bfloat16, jnp.float32
    dma = pltpu.SemaphoreType.DMA
    vmem = pl.BlockSpec(memory_space=pltpu.VMEM)
    hbm = pl.BlockSpec(memory_space=pl.ANY)
    flops = 2 * total * width * part * local_count * 3
    return pl.pallas_call(
        fused_kernel,
        out_shape=jax.ShapeDtypeStruct((T, width), bf16),
        in_specs=[hbm] * 6,
        out_specs=vmem,
        scratch_shapes=[
            pltpu.VMEM((total, width), bf16),
            pltpu.VMEM((total, LANES), f32),
            pltpu.VMEM((expert_ids.shape[1], T), jnp.int32),
            pltpu.VMEM((expert_ids.shape[1], T), f32),
            pltpu.VMEM(w_gate.shape, bf16),
            pltpu.VMEM(w_up.shape, bf16),
            pltpu.VMEM(w_down.shape, bf16),
            pltpu.VMEM((local_count, total, part), f32),
            pltpu.VMEM((local_count, total, part), f32),
            pltpu.VMEM((local_count, total, part), bf16),
            pltpu.VMEM((local_count, total, LANES), f32),
            pltpu.VMEM((half, width), f32),
            pltpu.VMEM((half, width), bf16),
            pltpu.VMEM((half, width), bf16),
            pltpu.VMEM((line, width), bf16),
            pltpu.VMEM((line, width), bf16),
            pltpu.VMEM((line, width), bf16),
            pltpu.VMEM((nz, T, width), bf16),
            *[dma] * 3,
            dma((steps,)),
            dma((steps,)),
            dma,
            *[dma((nz,)), dma((nz,)), dma((nz,)), dma((nz,)), dma((2,)), dma((2,))],
            *[dma((steps, nz))] * 4,
            *[dma((steps, 2))] * 2,
            *[dma((reduce_steps,))] * 4,
            *[dma((reduce_steps, nz))] * 2,
        ],
        compiler_params=pltpu.CompilerParams(
            collective_id=0, has_side_effects=True, vmem_limit_bytes=50 * 1024 * 1024
        ),
        cost_estimate=pl.CostEstimate(
            flops=flops,
            bytes_accessed=2 * (w_gate.size + w_up.size + w_down.size),
            transcendentals=total * part * local_count,
        ),
    )(tokens, expert_ids.T, gate_weights.T, w_gate, w_up, w_down)


def pick(mesh):
    def body(tokens, expert_ids, gate_weights, w_gate, w_up, w_down):
        expert_count = mesh.shape["expert"]
        rows = tokens.shape[0] * expert_count * mesh.shape["split"]
        fits = (
            mesh.shape["split"] == 2
            and expert_count % 2 == 0
            and rows <= 256
            and tokens.shape[0] % 16 == 0
            and tokens.shape[1] % GATHER == 0
            and tokens.shape[1] % REDUCE == 0
            and w_gate.shape[0] * expert_count <= LANES
        )
        run = fused_shards if fits else shards
        return run(tokens, expert_ids, gate_weights, w_gate, w_up, w_down)

    return body


def solution(mesh):
    in_specs = (
        P(("groups", "expert", "split"), None),
        P(("groups", "expert", "split"), None),
        P(("groups", "expert", "split"), None),
        P("expert", None, "split"),
        P("expert", None, "split"),
        P("expert", "split", None),
    )
    out_specs = P(("groups", "expert", "split"), None)
    return jax.shard_map(pick(mesh), mesh=mesh, in_specs=in_specs, out_specs=out_specs, check_vma=False)
```

```python
import jax
import jax.numpy as jnp
from jax import lax
from jax.experimental import pallas as pl
from jax.experimental.pallas import tpu as pltpu
from jax.sharding import PartitionSpec as P


def slot_targets(chosen_ids, capacity, expert_total):
    flat_ids = chosen_ids.reshape(-1)
    chosen = (flat_ids[:, None] == jnp.arange(expert_total, dtype=jnp.int32)[None, :]).astype(
        jnp.int32
    )
    earlier = jnp.cumsum(chosen, axis=0) - chosen
    slot_index = jnp.sum(earlier * chosen, axis=1)
    return (flat_ids * capacity + slot_index).reshape(chosen_ids.shape)


def shards(tokens, expert_ids, gate_weights, w_gate, w_up, w_down):
    expert_count = lax.axis_size("expert")
    local_count = w_gate.shape[0]
    expert_total = local_count * expert_count
    width = tokens.shape[1]
    capacity = max(3, tokens.shape[0] * expert_ids.shape[1] // expert_total)
    destination = slot_targets(expert_ids, capacity, expert_total)
    slot_range = jnp.arange(expert_total * capacity, dtype=jnp.int32)
    matches = slot_range[:, None, None] == destination[None, :, :]
    selector = jnp.any(matches, axis=-1).astype(jnp.bfloat16)
    send_buffer = jnp.dot(selector, tokens, preferred_element_type=jnp.float32).astype(jnp.bfloat16)
    send_buffer = send_buffer.reshape(expert_total, capacity, width)

    def run_experts(piece, start=0):
        block_shape = piece.shape
        row_block = piece.reshape(-1, local_count, capacity, width)
        gate_act = jnp.einsum(
            "mjcd,jdf->mjcf", row_block, w_gate, preferred_element_type=jnp.float32
        )
        up_act = jnp.einsum("mjcd,jdf->mjcf", row_block, w_up, preferred_element_type=jnp.float32)
        hidden = (jax.nn.silu(gate_act) * up_act).astype(jnp.bfloat16)
        partial_value = jnp.einsum(
            "mjcf,jfd->mjcd", hidden, w_down, preferred_element_type=jnp.float32
        )
        return partial_value.astype(jnp.bfloat16).reshape(block_shape)

    arrived = lax.all_to_all(send_buffer, "expert", split_axis=0, concat_axis=0, tiled=True)
    arrived = arrived.reshape(expert_count, 1, local_count, capacity, width)
    partial_value = run_experts(lax.all_gather(arrived, "split", axis=1, tiled=True), jnp.int32(0))
    summed = lax.psum_scatter(
        partial_value.astype(jnp.float32).astype(jnp.bfloat16),
        "split",
        scatter_dimension=1,
        tiled=True,
    )
    expert_out = summed.reshape(expert_total, capacity, width)
    returned = lax.all_to_all(expert_out, "expert", split_axis=0, concat_axis=0, tiled=True)
    combiner = jnp.sum(jnp.where(matches, gate_weights[None, :, :], 0.0), axis=-1).T
    mixed = jnp.dot(
        combiner,
        returned.reshape(expert_total * capacity, width).astype(jnp.float32),
        precision=lax.Precision.HIGHEST,
        preferred_element_type=jnp.float32,
    )
    return mixed.astype(jnp.bfloat16)


GATHER = 896
REDUCE = 896
AHEAD = 1
LAGS = (1, 2, 4)
LANES = 128


def fused_kernel(
    tok_hbm, ids_hbm, gw_hbm, wg_hbm, wu_hbm, wd_hbm, out_ref,
    xg, ext, ids_ref, gw_ref, wg, wu, wd, acc_g, acc_u, hid, cw, y, s1, r1, s2, r2, s3, r3,
    tok_sem, ids_sem, gw_sem, wg_sem, wu_sem, wd_sem,
    ezs, ezr, exs, exr, ecs, ecr,
    zs, zr, xs, xr, cs, cr,
    s1s, s1r, s2s, s2r, s3s, s3r,
):
    T, width = tok_hbm.shape
    local_count, _, part = wg.shape
    nz = lax.axis_size("expert") // 2
    steps, reduce_steps = width // GATHER, width // REDUCE
    line = nz * T
    half = 2 * line
    e_idx = lax.axis_index("expert")
    x_idx = lax.axis_index("split")
    z, core = e_idx // 2, lax.rem(e_idx, 2)
    core_peer = {"expert": z * 2 + (1 - core), "split": x_idx}
    x_peer = {"expert": e_idx, "split": 1 - x_idx}

    def z_at(offset):
        return lax.rem(z + (offset % nz), nz)

    def z_peer(offset):
        return {"expert": z_at(offset) * 2 + core, "split": x_idx}

    def cols(c, size=GATHER):
        return pl.ds(pl.multiple_of(c * size, size), size)

    def rows(index, base=0):
        return pl.ds(pl.multiple_of(base + index * T, T), T)

    def remote(src, dst, send, recv, peer):
        return pltpu.make_async_remote_copy(
            src_ref=src, dst_ref=dst, send_sem=send, recv_sem=recv,
            device_id=peer, device_id_type=pl.DeviceIdType.MESH,
        )

    own = rows(z)
    tok_copy = pltpu.make_async_copy(tok_hbm, xg.at[own, :], tok_sem)
    ids_copy = pltpu.make_async_copy(ids_hbm, ids_ref, ids_sem)
    gw_copy = pltpu.make_async_copy(gw_hbm, gw_ref, gw_sem)
    for copy in (ids_copy, gw_copy, tok_copy):
        copy.start()

    def w_copy(c):
        return (
            pltpu.make_async_copy(wg_hbm.at[:, cols(c), :], wg.at[:, cols(c), :], wg_sem.at[c]),
            pltpu.make_async_copy(wu_hbm.at[:, cols(c), :], wu.at[:, cols(c), :], wu_sem.at[c]),
        )

    wd_copy = pltpu.make_async_copy(wd_hbm, wd, wd_sem)

    barrier = pltpu.get_barrier_semaphore()
    peers = [core_peer, x_peer] + [z_peer(d) for d in range(1, nz)]
    for peer in peers:
        pl.semaphore_signal(barrier, inc=1, device_id=peer, device_id_type=pl.DeviceIdType.MESH)

    @pl.loop(0, steps)
    def _(c):
        for copy in w_copy(c):
            copy.start()

    wd_copy.start()

    acc_g[...] = jnp.zeros_like(acc_g)
    acc_u[...] = jnp.zeros_like(acc_u)
    ids_copy.wait()
    gw_copy.wait()
    ids, weights = jnp.transpose(ids_ref[...]), jnp.transpose(gw_ref[...])
    lane = lax.broadcasted_iota(jnp.int32, (T, LANES), 1)
    table = jnp.zeros((T, LANES), jnp.float32)
    for k in range(ids.shape[1]):
        table = table + jnp.where(ids[:, k : k + 1] == lane, weights[:, k : k + 1], 0.0)
    ext[own, :] = table
    tok_copy.wait()
    pl.semaphore_wait(barrier, len(peers))

    def gz(buf, where, send, recv, d, arriving):
        block = buf.at[(rows(z_at(-d)) if arriving else own,) + where]
        return remote(block, block, send.at[d], recv.at[d], z_peer(d))

    def gx(buf, where, send, recv, d, arriving):
        index = z_at(-d)
        src = buf.at[(rows(index),) + where]
        dst = buf.at[(rows(index, line),) + where]
        if arriving:
            src = dst
        return remote(src, dst, send.at[d], recv.at[d], x_peer)

    def gc(buf, where, send, recv, side, arriving):
        src = buf.at[(pl.ds(side * line, line),) + where]
        dst = buf.at[(pl.ds(half + side * line, line),) + where]
        if arriving:
            src = dst
        return remote(src, dst, send.at[side], recv.at[side], core_peer)

    e_where = (slice(None),)

    def e_args(send, recv):
        return ext, e_where, send, recv

    def c_args(c, send, recv):
        return xg, (cols(c),), send.at[c], recv.at[c]

    near_first = sorted(range(1, nz), key=lambda d: min(d, nz - d))

    def first_sends(za, xa):
        gx(*xa, 0, False).start()
        for d in near_first:
            gz(*za, d, False).start()

    def forward_line(za, xa, ca):
        for d in near_first:
            gz(*za, d, True).wait_recv()
            gx(*xa, d, False).start()
        gc(*ca, 0, False).start()

    def forward_other(xa, ca):
        for d in range(nz):
            gx(*xa, d, True).wait_recv()
        gc(*ca, 1, False).start()

    def from_core(ca):
        for side in range(2):
            gc(*ca, side, True).wait_recv()

    def gather_sent(za, xa, ca):
        for d in range(1, nz):
            gz(*za, d, False).wait_send()
        for d in range(nz):
            gx(*xa, d, False).wait_send()
        for side in range(2):
            gc(*ca, side, False).wait_send()

    ez, ex, ec = e_args(ezs, ezr), e_args(exs, exr), e_args(ecs, ecr)
    first_sends(ez, ex)

    for c in range(AHEAD):
        first_sends(c_args(c, zs, zr), c_args(c, xs, xr))
    forward_line(ez, ex, ec)

    @pl.loop(0, steps + 2)
    def _(i):
        @pl.when(i + AHEAD < steps)
        def _():
            first_sends(c_args(i + AHEAD, zs, zr), c_args(i + AHEAD, xs, xr))

        @pl.when(i < steps)
        def _():
            forward_line(c_args(i, zs, zr), c_args(i, xs, xr), c_args(i, cs, cr))

        @pl.when((i >= 1) & (i < steps + 1))
        def _():
            forward_other(c_args(i - 1, xs, xr), c_args(i - 1, cs, cr))

        @pl.when(i == 1)
        def _():
            forward_other(ex, ec)

        @pl.when(i == 2)
        def _():
            from_core(ec)
            lanes = lax.broadcasted_iota(jnp.int32, (2 * half, LANES), 1)
            for j in range(local_count):
                chosen = jnp.where(lanes == e_idx * local_count + j, ext[...], 0.0)
                weight = jnp.sum(chosen, axis=1, keepdims=True)
                cw[j] = jnp.broadcast_to(weight, (2 * half, LANES))

        @pl.when(i >= 2)
        def _():
            c = i - 2
            from_core(c_args(c, cs, cr))
            for copy in w_copy(c):
                copy.wait()
            value = xg[:, cols(c)]
            for j in range(local_count):
                acc_g[j] += jnp.dot(value, wg[j, cols(c), :], preferred_element_type=jnp.float32)
                acc_u[j] += jnp.dot(value, wu[j, cols(c), :], preferred_element_type=jnp.float32)

    for j in range(local_count):
        gate = acc_g[j]
        hid[j] = (gate / (1.0 + jnp.exp(-gate)) * acc_u[j]).astype(jnp.bfloat16)
    wd_copy.wait()

    def rc(c):
        return remote(s1.at[:, cols(c, REDUCE)], r1.at[:, cols(c, REDUCE)], s1s.at[c], s1r.at[c], core_peer)

    def rx(c):
        return remote(s2.at[:, cols(c, REDUCE)], r2.at[:, cols(c, REDUCE)], s2s.at[c], s2r.at[c], x_peer)

    def rz(c, d):
        return remote(
            s3.at[rows(z_at(d)), cols(c, REDUCE)], r3.at[d, :, cols(c, REDUCE)],
            s3s.at[c, d], s3r.at[c, d], z_peer(d),
        )

    lag_x, lag_z, lag_out = LAGS

    @pl.loop(0, reduce_steps + lag_out)
    def _(i):
        @pl.when(i < reduce_steps)
        def _():
            total = None
            for j in range(local_count):
                value = jnp.dot(hid[j], wd[j, :, cols(i, REDUCE)], preferred_element_type=jnp.float32)
                value = value * jnp.concatenate([cw[j]] * (REDUCE // LANES), axis=1)
                total = value if total is None else total + value
            s1[:, cols(i, REDUCE)] = total[half:].astype(jnp.bfloat16)
            y[:, cols(i, REDUCE)] = total[:half]
            rc(i).start()

        @pl.when((i >= lag_x) & (i < reduce_steps + lag_x))
        def _():
            c = i - lag_x
            rc(c).wait_recv()
            total = y[:, cols(c, REDUCE)] + r1[:, cols(c, REDUCE)].astype(jnp.float32)
            s2[:, cols(c, REDUCE)] = total[line:].astype(jnp.bfloat16)
            y[:line, cols(c, REDUCE)] = total[:line]
            rx(c).start()

        @pl.when((i >= lag_z) & (i < reduce_steps + lag_z))
        def _():
            c = i - lag_z
            rx(c).wait_recv()
            total = y[:line, cols(c, REDUCE)] + r2[:, cols(c, REDUCE)].astype(jnp.float32)
            s3[:, cols(c, REDUCE)] = total.astype(jnp.bfloat16)
            y[:line, cols(c, REDUCE)] = total
            for d in range(1, nz):
                rz(c, d).start()

        @pl.when(i >= lag_out)
        def _():
            c = i - lag_out
            total = y[own, cols(c, REDUCE)]
            for d in range(1, nz):
                rz(c, d).wait_recv()
                total = total + r3[d, :, cols(c, REDUCE)].astype(jnp.float32)
            out_ref[:, cols(c, REDUCE)] = total.astype(out_ref.dtype)
            rc(c).wait_send()
            rx(c).wait_send()
            for d in range(1, nz):
                rz(c, d).wait_send()

        @pl.when(i < steps)
        def _():
            gather_sent(c_args(i, zs, zr), c_args(i, xs, xr), c_args(i, cs, cr))

    gather_sent(ez, ex, ec)


def fused_shards(tokens, expert_ids, gate_weights, w_gate, w_up, w_down):
    T, width = tokens.shape
    local_count, _, part = w_gate.shape
    nz = lax.axis_size("expert") // 2
    steps, reduce_steps = width // GATHER, width // REDUCE
    line = nz * T
    half, total = 2 * line, 4 * line
    bf16, f32 = jnp.bfloat16, jnp.float32
    dma = pltpu.SemaphoreType.DMA
    vmem = pl.BlockSpec(memory_space=pltpu.VMEM)
    hbm = pl.BlockSpec(memory_space=pl.ANY)
    flops = 2 * total * width * part * local_count * 3
    return pl.pallas_call(
        fused_kernel,
        out_shape=jax.ShapeDtypeStruct((T, width), bf16),
        in_specs=[hbm] * 6,
        out_specs=vmem,
        scratch_shapes=[
            pltpu.VMEM((total, width), bf16),
            pltpu.VMEM((total, LANES), f32),
            pltpu.VMEM((expert_ids.shape[1], T), jnp.int32),
            pltpu.VMEM((expert_ids.shape[1], T), f32),
            pltpu.VMEM(w_gate.shape, bf16),
            pltpu.VMEM(w_up.shape, bf16),
            pltpu.VMEM(w_down.shape, bf16),
            pltpu.VMEM((local_count, total, part), f32),
            pltpu.VMEM((local_count, total, part), f32),
            pltpu.VMEM((local_count, total, part), bf16),
            pltpu.VMEM((local_count, total, LANES), f32),
            pltpu.VMEM((half, width), f32),
            pltpu.VMEM((half, width), bf16),
            pltpu.VMEM((half, width), bf16),
            pltpu.VMEM((line, width), bf16),
            pltpu.VMEM((line, width), bf16),
            pltpu.VMEM((line, width), bf16),
            pltpu.VMEM((nz, T, width), bf16),
            *[dma] * 3,
            dma((steps,)),
            dma((steps,)),
            dma,
            *[dma((nz,)), dma((nz,)), dma((nz,)), dma((nz,)), dma((2,)), dma((2,))],
            *[dma((steps, nz))] * 4,
            *[dma((steps, 2))] * 2,
            *[dma((reduce_steps,))] * 4,
            *[dma((reduce_steps, nz))] * 2,
        ],
        compiler_params=pltpu.CompilerParams(
            collective_id=0, has_side_effects=True, vmem_limit_bytes=50 * 1024 * 1024
        ),
        cost_estimate=pl.CostEstimate(
            flops=flops,
            bytes_accessed=2 * (w_gate.size + w_up.size + w_down.size),
            transcendentals=total * part * local_count,
        ),
    )(tokens, expert_ids.T, gate_weights.T, w_gate, w_up, w_down)


def pick(mesh):
    def body(tokens, expert_ids, gate_weights, w_gate, w_up, w_down):
        expert_count = mesh.shape["expert"]
        rows = tokens.shape[0] * expert_count * mesh.shape["split"]
        fits = (
            mesh.shape["split"] == 2
            and expert_count % 2 == 0
            and rows <= 256
            and tokens.shape[0] % 16 == 0
            and tokens.shape[1] % GATHER == 0
            and tokens.shape[1] % REDUCE == 0
            and w_gate.shape[0] * expert_count <= LANES
        )
        run = fused_shards if fits else shards
        return run(tokens, expert_ids, gate_weights, w_gate, w_up, w_down)

    return body


def solution(mesh):
    in_specs = (
        P(("groups", "expert", "split"), None),
        P(("groups", "expert", "split"), None),
        P(("groups", "expert", "split"), None),
        P("expert", None, "split"),
        P("expert", None, "split"),
        P("expert", "split", None),
    )
    out_specs = P(("groups", "expert", "split"), None)
    return jax.shard_map(pick(mesh), mesh=mesh, in_specs=in_specs, out_specs=out_specs, check_vma=False)
```
